32 devices in a mesh: blocks: 8 (over z, x), chan: 4 (over y, core).
Axes of the slice: x: 2, y: 2, z: 4, core: 2. Of those that a mesh axis runs over, the one named last changes fastest.
Arguments:
- fine_input: bfloat16 [128, 64, 512], P('blocks', 'chan'), may hold values from -6 to 6
- block_counts: int32 [8], replicated, may hold values from 8 to 16, as said below
- fine_weight: bfloat16 [7, 64, 64], P(None, 'chan'), may hold values from -0.25 to 0.25
- fine_bias: float32 [64], P('chan'), may hold values from -3 to 3
- coarse_weight: bfloat16 [7, 64, 64], P(None, 'chan'), may hold values from -0.25 to 0.25
- coarse_bias: float32 [64], P('chan'), may hold values from -3 to 3
- coarse_cotangent: bfloat16 [16, 64, 512], P('blocks', 'chan'), may hold values from -48 to 48
Outputs:
- coarser_level_output: bfloat16 [16, 64, 512], P('blocks', 'chan')
- fine_grad: bfloat16 [128, 64, 512], P('blocks', 'chan')
- fine_weight_grad: float32 [7, 64, 64], P(None, 'chan')
- fine_bias_grad: float32 [64], P('chan')
- coarse_weight_grad: float32 [7, 64, 64], P(None, 'chan')
- coarse_bias_grad: float32 [64], P('chan')
The draws below stay inside these ranges and needn't reach their ends.
Inputs may be any that keep to these rules, and one draw needn't show every extreme that they name: `block_counts`: fine blocks held by each device of blocks; they sum to 96, and some device holds exactly 16.
All inputs are finite; a program needn't handle non-finite values.
Results may differ from the reference program's by a relative error of at most 0.017.
Values may be sent and summed in bfloat16 or wider, within the bound.
A program may use at most 64 MiB of HBM per device.

```python
import math
import jax
import jax.numpy as jnp
from jax import lax

C = 64
EDGE = 8
SLOTS_F = 16
SLOTS_C = 2
NFINE = 96
NCOARSE = 12
N_BLOCKS = 8


def draw_block_counts(key, part):
    half_count = N_BLOCKS // 2
    spare = SLOTS_F - 8
    first_key, second_key, third_key = jax.random.split(key, 3)
    extra = jax.random.randint(first_key, (half_count,), 0, spare + 1)
    forced = jax.random.randint(second_key, (), 0, half_count)
    extra = jnp.where(jnp.arange(half_count) == forced, spare, extra)
    paired = jnp.concatenate([extra, spare - extra])
    shuffle = jax.random.permutation(third_key, N_BLOCKS)
    return (8 + paired[shuffle]).astype(jnp.int32)


def levels(own_key, dims, pieces, least, top_value):
    loudness = 1.0
    for dim, blocks in pieces:
        steps = jax.random.uniform(jax.random.fold_in(jax.random.fold_in(own_key, 6), dim), (blocks,), jnp.float32, least / len(pieces), top_value / len(pieces))
        loudness = loudness * jnp.repeat(jnp.exp(steps), dims[dim] // blocks).reshape((-1,) + (1,) * (len(dims) - 1 - dim))
    return loudness


def gaussian(own_key, extent, scale, reach, pieces=(), kind=jnp.bfloat16):
    drawn = scale * jax.random.normal(own_key, extent, jnp.float32)
    if pieces:
        drawn = drawn * levels(own_key, extent, pieces, -0.22, 0.18)
    return jnp.clip(drawn, -reach, reach).astype(kind)


def setup_inputs(seed: int = 0) -> dict:
    arg_keys = jax.random.split(jax.random.key(seed), 8)
    return {
        "fine_input": gaussian(arg_keys[0], (N_BLOCKS * SLOTS_F, C, EDGE ** 3), 1.0, 6.0, ((0, 8), (1, 4))),
        "block_counts": draw_block_counts(jax.random.fold_in(arg_keys[7], 71), 0),
        "fine_weight": gaussian(arg_keys[2], (7, C, C), (7 * C) ** -0.5, 0.25, ((1, 4),)),
        "fine_bias": gaussian(arg_keys[3], (C,), 0.5, 3.0, ((0, 4),), jnp.float32),
        "coarse_weight": gaussian(arg_keys[4], (7, C, C), (7 * C) ** -0.5, 0.25, ((1, 4),)),
        "coarse_bias": gaussian(arg_keys[5], (C,), 0.5, 3.0, ((0, 4),), jnp.float32),
        "coarse_cotangent": gaussian(arg_keys[6], (N_BLOCKS * SLOTS_C, C, EDGE ** 3), 8.0, 48.0, ((0, 8), (1, 4))),
    }


TAP_PAIRS = (0, 2, 1, 4, 3, 6, 5)

def block_layers(block_cube):
    channels, edge_cells = (block_cube.shape[0], block_cube.shape[1])
    side_layers = [block_cube[:, :, :, 0], block_cube[:, :, :, -1], block_cube[:, :, 0, :], block_cube[:, :, -1, :], block_cube[:, 0], block_cube[:, -1]]
    return jnp.stack(side_layers).reshape(6, channels, edge_cells * edge_cells)

def block_views(block_cube, halo_layers):
    channels, edge_cells = (block_cube.shape[0], block_cube.shape[1])
    sheets = halo_layers.reshape(6, channels, edge_cells, edge_cells)
    minus_x = jnp.concatenate([sheets[0][:, :, :, None], block_cube[:, :, :, :-1]], axis=3)
    plus_x = jnp.concatenate([block_cube[:, :, :, 1:], sheets[1][:, :, :, None]], axis=3)
    minus_y = jnp.concatenate([sheets[2][:, :, None, :], block_cube[:, :, :-1, :]], axis=2)
    plus_y = jnp.concatenate([block_cube[:, :, 1:, :], sheets[3][:, :, None, :]], axis=2)
    minus_z = jnp.concatenate([sheets[4][:, None], block_cube[:, :-1]], axis=1)
    plus_z = jnp.concatenate([block_cube[:, 1:], sheets[5][:, None]], axis=1)
    stacked = jnp.stack([block_cube, minus_x, plus_x, minus_y, plus_y, minus_z, plus_z])
    return stacked.reshape(7 * channels, edge_cells ** 3)

def slope_of(pre_values):
    sigmoid_values = jax.nn.sigmoid(pre_values)
    return sigmoid_values * (1.0 + pre_values * (1.0 - sigmoid_values))

def fine_halos(layer_table, total_blocks):
    block_ids = jnp.arange(total_blocks, dtype=jnp.int32)
    offsets = jnp.array([-1, 1, -2, 2, -4, 4], jnp.int32)
    facing = jnp.array([1, 0, 3, 2, 5, 4], jnp.int32)
    parity_x = block_ids % 2
    parity_y = block_ids // 2 % 2
    keep_mask = jnp.stack([parity_x == 1, parity_x == 0, parity_y == 1, parity_y == 0, block_ids >= 4, block_ids + 4 < total_blocks], axis=1)
    neighbour = jnp.clip(block_ids[:, None] + offsets[None, :], 0, total_blocks - 1).astype(jnp.int32)
    fetched = layer_table[neighbour, facing[None, :]]
    return jnp.where(keep_mask[:, :, None, None], fetched, jnp.zeros((), layer_table.dtype))

def coarse_halos(layer_table, total_blocks):
    coarse_ids = jnp.arange(total_blocks, dtype=jnp.int32)
    zero_value = jnp.zeros((), layer_table.dtype)
    lower_rows = jnp.clip(coarse_ids - 1, 0, total_blocks - 1).astype(jnp.int32)
    upper_rows = jnp.clip(coarse_ids + 1, 0, total_blocks - 1).astype(jnp.int32)
    below_layer = jnp.where((coarse_ids >= 1)[:, None, None], layer_table[lower_rows, 5], zero_value)
    above_layer = jnp.where((coarse_ids + 1 < total_blocks)[:, None, None], layer_table[upper_rows, 4], zero_value)
    flat_zero = jnp.zeros_like(below_layer)
    return jnp.stack([flat_zero, flat_zero, flat_zero, flat_zero, below_layer, above_layer], axis=1)

def apply_blocks(matrix, block_cubes, halo_table):

    def one_block(operands):
        return jnp.dot(matrix, block_views(operands[0], operands[1]), preferred_element_type=jnp.float32)
    return lax.map(one_block, (block_cubes, halo_table))

def weight_terms(block_cubes, halo_table, deltas):

    def one_block(operands):
        tap_views = block_views(operands[0], operands[1])
        return lax.dot_general(operands[2], tap_views, (((1,), (1,)), ((), ())), preferred_element_type=jnp.float32)
    summed = lax.optimization_barrier(jnp.sum(lax.map(one_block, (block_cubes, halo_table, deltas)), axis=0))
    return summed.reshape(C, 7, C).transpose(1, 0, 2)

def reference(fine_input, block_counts, fine_weight, fine_bias, coarse_weight, coarse_bias, coarse_cotangent):
    cell_count = EDGE ** 3
    half_edge = EDGE // 2
    starts = (jnp.cumsum(block_counts) - block_counts).astype(jnp.int32)
    block_ids = jnp.arange(NFINE, dtype=jnp.int32)
    owners = (lax.optimization_barrier(jnp.sum((starts[None, :] <= block_ids[:, None]).astype(jnp.int32), axis=1)) - 1).astype(jnp.int32)
    finer_level_slots = (owners * SLOTS_F + block_ids - starts[owners]).astype(jnp.int32)
    coarse_ids = jnp.arange(NCOARSE, dtype=jnp.int32)
    coarse_owners = owners[coarse_ids * 8]
    coarse_slots = (coarse_owners * SLOTS_C + coarse_ids - (starts[coarse_owners] + 7) // 8).astype(jnp.int32)
    pair_index = jnp.array(TAP_PAIRS, jnp.int32)
    fine_cubes = fine_input[finer_level_slots].reshape(NFINE, C, EDGE, EDGE, EDGE)
    input_halos = fine_halos(jax.vmap(block_layers)(fine_cubes), NFINE)
    forward_fine = fine_weight.transpose(1, 0, 2).reshape(C, 7 * C)
    pre_fine = apply_blocks(forward_fine, fine_cubes, input_halos) + fine_bias.astype(jnp.float32)[None, :, None]
    hidden = jax.nn.silu(pre_fine).astype(jnp.bfloat16)
    shaped = hidden.reshape(NFINE, C, half_edge, 2, half_edge, 2, half_edge, 2)
    octants = (lax.optimization_barrier(jnp.sum(shaped, axis=(3, 5, 7), dtype=jnp.float32)) * 0.125).astype(jnp.bfloat16)
    coarse_input = octants.reshape(NCOARSE, 2, 2, 2, C, half_edge, half_edge, half_edge).transpose(0, 4, 1, 5, 2, 6, 3, 7).reshape(NCOARSE, C, cell_count)
    coarse_cubes = coarse_input.reshape(NCOARSE, C, EDGE, EDGE, EDGE)
    coarse_in_halos = coarse_halos(jax.vmap(block_layers)(coarse_cubes), NCOARSE)
    forward_coarser_level = coarse_weight.transpose(1, 0, 2).reshape(C, 7 * C)
    pre_coarse = apply_blocks(forward_coarser_level, coarse_cubes, coarse_in_halos) + coarse_bias.astype(jnp.float32)[None, :, None]
    coarse_values = jax.nn.silu(pre_coarse).astype(jnp.bfloat16)
    cotangent = coarse_cotangent[coarse_slots].astype(jnp.float32)
    coarser_level_delta = (cotangent * slope_of(pre_coarse)).astype(jnp.bfloat16)
    coarse_norm = math.sqrt(NCOARSE * cell_count)
    coarse_weight_grad = weight_terms(coarse_cubes, coarse_in_halos, coarser_level_delta) / coarse_norm
    coarse_bias_grad = lax.optimization_barrier(jnp.sum(coarser_level_delta.astype(jnp.float32), axis=(0, 2))) / coarse_norm
    delta_cubes = coarser_level_delta.reshape(NCOARSE, C, EDGE, EDGE, EDGE)
    delta_halos = coarse_halos(jax.vmap(block_layers)(delta_cubes), NCOARSE)
    backward_coarser_level = coarse_weight[pair_index].transpose(2, 0, 1).reshape(C, 7 * C)
    coarse_back = apply_blocks(backward_coarser_level, delta_cubes, delta_halos).astype(jnp.bfloat16)
    coarse_octants = coarse_back.reshape(NCOARSE, C, 2, half_edge, 2, half_edge, 2, half_edge).transpose(0, 2, 4, 6, 1, 3, 5, 7).reshape(NFINE, C, half_edge, 1, half_edge, 1, half_edge, 1)
    widened = jnp.broadcast_to(coarse_octants, (NFINE, C, half_edge, 2, half_edge, 2, half_edge, 2)).reshape(NFINE, C, cell_count)
    fine_delta = (widened.astype(jnp.float32) * 0.125 * slope_of(pre_fine)).astype(jnp.bfloat16)
    fine_norm = math.sqrt(NFINE * cell_count)
    fine_weight_grad = weight_terms(fine_cubes, input_halos, fine_delta) / fine_norm
    fine_bias_grad = lax.optimization_barrier(jnp.sum(fine_delta.astype(jnp.float32), axis=(0, 2))) / fine_norm
    fine_delta_cubes = fine_delta.reshape(NFINE, C, EDGE, EDGE, EDGE)
    fine_delta_halos = fine_halos(jax.vmap(block_layers)(fine_delta_cubes), NFINE)
    back_fine = fine_weight[pair_index].transpose(2, 0, 1).reshape(C, 7 * C)
    fine_back = apply_blocks(back_fine, fine_delta_cubes, fine_delta_halos).astype(jnp.bfloat16)
    coarser_level_output = jnp.zeros((N_BLOCKS * SLOTS_C, C, cell_count), jnp.bfloat16).at[coarse_slots].set(coarse_values)
    fine_grad = jnp.zeros((N_BLOCKS * SLOTS_F, C, cell_count), jnp.bfloat16).at[finer_level_slots].set(fine_back)
    return (coarser_level_output, fine_grad, fine_weight_grad, fine_bias_grad, coarse_weight_grad, coarse_bias_grad)
```

```python
import jax
import jax.numpy as jnp
import numpy as np
from jax import lax
from jax.experimental import pallas as pl
from jax.experimental.pallas import tpu as pltpu
from jax.sharding import PartitionSpec as P

EDGE = 8
CELLS = EDGE**3
TAP_PAIRS = (0, 2, 1, 4, 3, 6, 5)
STRIDES = (1, 8, 64)
F32 = jnp.float32
BF16 = jnp.bfloat16


def from_behind(block, axis, distance):
    devices = range(lax.axis_size(axis))
    route = [(i - distance, i) for i in devices if i - distance in devices]
    return lax.ppermute(block, axis, route)


def octant_maps():
    z, y, x = np.meshgrid(*[np.arange(EDGE)] * 3, indexing="ij")
    spread = np.zeros((8, CELLS, CELLS), np.float32)
    pool = np.zeros((CELLS, 64), np.float32)
    place = np.zeros((8, 64, CELLS), np.float32)
    fine = np.arange(CELLS)
    small = ((z // 2) * 16 + (y // 2) * 4 + x // 2).reshape(-1)
    pool[fine, small] = 1.0
    for q in range(8):
        cz, cy, cx = z // 2 + 4 * (q // 4), y // 2 + 4 * (q // 2 % 2), x // 2 + 4 * (q % 2)
        coarse = (cz * 64 + cy * 8 + cx).reshape(-1)
        spread[q, coarse, fine] = 1.0
        place[q, small, coarse] = 1.0
    return spread, pool, place


def paired(taps):
    return jnp.stack([taps[t] for t in TAP_PAIRS])


def sigmoid(v):
    return 1.0 / (1.0 + jnp.exp(-v))


def write_views(views, own, neighbours, width):
    lane = lax.broadcasted_iota(jnp.int32, own.shape, 1)
    views[0:width, :] = own
    wide = own.astype(F32)
    for axis in range(3):
        stride = STRIDES[axis]
        coord = lane // stride % EDGE
        for side in range(2):
            near, far = (0, EDGE - 1) if side == 0 else (EDGE - 1, 0)
            step = stride if side == 0 else CELLS - stride
            wrap = (CELLS - 7 * stride) if side == 0 else 7 * stride
            tap = 1 + 2 * axis + side
            other = neighbours[2 * axis + side]
            if other is None:
                out = jnp.where(coord == near, 0.0, pltpu.roll(wide, step, 1))
            else:
                mixed = jnp.where(coord == far, other.astype(F32), wide)
                out = pltpu.roll(mixed, step, 1)
                if step != wrap % CELLS:
                    out = jnp.where(coord == near, pltpu.roll(mixed, wrap, 1), out)
            views[tap * width : (tap + 1) * width, :] = out.astype(BF16)


def forward_kernel(near, table, weight, bias, pool, slope, octants, views):
    width = table.shape[1]

    def row(j, carry):
        own = table[j + 4]
        write_views(views, own, [table[near[j * 6 + n]] for n in range(6)], width)
        v = jnp.dot(weight[...], views[...], preferred_element_type=F32) + bias[...]
        s = sigmoid(v)
        slope[j] = s * (1.0 + v * (1.0 - s))

        @pl.when(jnp.logical_and(j >= 4, j < 20))
        def _():
            hidden = (v * s).astype(BF16)
            small = jnp.dot(hidden, pool[...], preferred_element_type=F32) * 0.125
            octants[j - 4] = small.astype(BF16)

        return carry

    lax.fori_loop(0, slope.shape[0], row, 0)


def backward_kernel(
    near, facts, octant_at, cotangent_at, table, slope, octants, cotangent, forward_w, coarse_b, back_coarse_w, back_w,
    place, spread,
    coarse_out, fine_grad, fine_wg, fine_bg, coarse_wg, coarse_bg,
    views, coarse_in, coarse_act, coarse_delta, coarse_back, fine_delta, bias_sum,
):
    width = table.shape[1]
    group = fine_grad.shape[1]
    chan, live, parent0, coarse_row, coarse_live = (facts[n] for n in range(5))
    mine = pl.ds(pl.multiple_of(chan * group, group), group)

    def own_views():
        return jnp.concatenate(
            [views[pl.ds(pl.multiple_of(t * width + chan * group, group), group), :] for t in range(7)],
            axis=0,
        )

    def assemble(k, carry):
        total = jnp.zeros((width, CELLS), F32)
        for q in range(8):
            total += jnp.dot(
                octants[octant_at[k * 8 + q]], place[q], preferred_element_type=F32
            )
        inside = jnp.logical_and(k >= facts[5], k < facts[6])
        coarse_in[k] = jnp.where(inside, total, 0.0).astype(BF16)
        return carry

    lax.fori_loop(0, 8, assemble, 0)

    def coarse_forward(k, carry):
        write_views(
            views, coarse_in[k + 1], [None] * 4 + [coarse_in[k], coarse_in[k + 2]], width
        )
        v = jnp.dot(forward_w[...], views[...], preferred_element_type=F32) + coarse_b[...]
        s = sigmoid(v)
        coarse_act[k] = (v * s).astype(BF16)
        inside = jnp.logical_and(k + 1 >= facts[5], k + 1 < facts[6])
        delta = cotangent[cotangent_at[k]].astype(F32) * (s * (1.0 + v * (1.0 - s)))
        coarse_delta[k] = jnp.where(inside, delta, 0.0).astype(BF16)
        return carry

    lax.fori_loop(0, 6, coarse_forward, 0)
    for s in range(coarse_out.shape[0]):
        row = jnp.minimum(coarse_row + s, 5)
        kept = jnp.where(s < coarse_live, coarse_act[row, mine, :].astype(F32), 0.0)
        coarse_out[s] = kept.astype(BF16)

    coarse_wg[...] = jnp.zeros_like(coarse_wg)
    bias_sum[...] = jnp.zeros_like(bias_sum)

    def coarse_backward(k, carry):
        write_views(
            views,
            coarse_delta[k + 1],
            [None] * 4 + [coarse_delta[k], coarse_delta[k + 2]],
            width,
        )
        coarse_back[k] = jnp.dot(
            back_coarse_w[...], views[...], preferred_element_type=F32
        ).astype(BF16)
        row = k + 1

        @pl.when(jnp.logical_and(row >= coarse_row, row < coarse_row + coarse_live))
        def _():
            coarse_wg[...] += lax.dot_general(
                own_views(), coarse_in[k + 2], (((1,), (1,)), ((), ())), preferred_element_type=F32
            )
            bias_sum[...] += coarse_delta[row, mine, :].astype(F32)

        return carry

    lax.fori_loop(0, 4, coarse_backward, 0)
    coarse_bg[...] = jnp.broadcast_to(
        jnp.sum(bias_sum[...], axis=1, keepdims=True), coarse_bg.shape
    )

    def delta_row(j, carry):
        index = parent0 + j
        up = jnp.dot(coarse_back[index // 8], spread[index % 8], preferred_element_type=F32)
        fine_delta[j] = (up * 0.125 * slope[j]).astype(BF16)
        return carry

    lax.fori_loop(0, slope.shape[0], delta_row, 0)
    fine_delta[slope.shape[0]] = jnp.zeros((width, CELLS), BF16)
    fine_wg[...] = jnp.zeros_like(fine_wg)
    bias_sum[...] = jnp.zeros_like(bias_sum)

    def fine_row(r, carry):
        @pl.when(r < live)
        def _():
            write_views(
                views, fine_delta[r + 4], [fine_delta[near[r * 6 + n]] for n in range(6)], width
            )
            fine_grad[r] = jnp.dot(back_w[...], views[...], preferred_element_type=F32).astype(BF16)
            fine_wg[...] += lax.dot_general(
                own_views(), table[r + 8], (((1,), (1,)), ((), ())), preferred_element_type=F32
            )
            bias_sum[...] += fine_delta[r + 4, mine, :].astype(F32)

        @pl.when(r >= live)
        def _():
            fine_grad[r] = jnp.zeros((group, CELLS), BF16)

        return carry

    lax.fori_loop(0, fine_grad.shape[0], fine_row, 0)
    fine_bg[...] = jnp.broadcast_to(jnp.sum(bias_sum[...], axis=1, keepdims=True), fine_bg.shape)


def local(
    fine_input, block_counts, fine_weight, fine_bias, coarse_weight, coarse_bias, coarse_cotangent
):
    slots, group, cells = fine_input.shape
    coarse_slots = coarse_cotangent.shape[0]
    channels = fine_weight.shape[2]
    device = lax.axis_index("blocks")
    chan = lax.axis_index("chan")
    order = jnp.arange(block_counts.shape[0])
    earlier = order[None, :] < order[:, None]
    starts = jnp.sum(jnp.where(earlier, block_counts[None, :], 0), axis=1)
    first = starts[device]
    live = block_counts[device]
    total = jnp.sum(block_counts)
    coarse_total = total // 8
    coarse_first = (first + 7) // 8
    coarse_count = (first + live + 7) // 8 - coarse_first

    lower = from_behind(lax.dynamic_slice_in_dim(fine_input, live - 8, 8, 0), "blocks", 1)
    upper = from_behind(fine_input[:8], "blocks", -1)
    rows = slots + 16
    table = jnp.concatenate([lower, fine_input, jnp.zeros((9, group, cells), BF16)], axis=0)
    table = lax.dynamic_update_slice_in_dim(table, upper, 8 + live, 0)
    table = lax.all_gather(table, "chan", axis=1, tiled=True)
    weights = lax.all_gather(
        jnp.concatenate([fine_weight, coarse_weight]), "chan", axis=1, tiled=True
    )
    biases = lax.all_gather(jnp.stack([fine_bias, coarse_bias]), "chan", axis=1, tiled=True)
    cotangents = lax.all_gather(
        lax.all_gather(coarse_cotangent, "chan", axis=1, tiled=True), "blocks", axis=0, tiled=True
    )
    full_fine, full_coarse = weights[:7], weights[7:]

    spread, pool, place = (jnp.asarray(a, BF16) for a in octant_maps())
    delta_rows = slots + 8
    ids = first - 4 + jnp.arange(delta_rows, dtype=jnp.int32)
    px, py = ids % 2, ids // 2 % 2
    valid = jnp.stack(
        [px == 1, px == 0, py == 1, py == 0, ids >= 4, ids + 4 < total], axis=1
    )
    offsets = jnp.array([-1, 1, -2, 2, -4, 4], jnp.int32)[None, :]
    spot = jnp.arange(delta_rows, dtype=jnp.int32)[:, None] + offsets
    near_fine = jnp.where(valid, spot + 4, rows).reshape(-1)
    near_delta = jnp.where(valid, spot, delta_rows)[4 : 4 + slots].reshape(-1)

    smem = pl.BlockSpec(memory_space=pltpu.SMEM)
    vmem = pl.BlockSpec(memory_space=pltpu.VMEM)
    slope, octants = pl.pallas_call(
        forward_kernel,
        out_shape=(
            jax.ShapeDtypeStruct((delta_rows, channels, cells), F32),
            jax.ShapeDtypeStruct((slots, channels, 64), BF16),
        ),
        in_specs=[smem] + [vmem] * 4,
        out_specs=(vmem, vmem),
        scratch_shapes=[pltpu.VMEM((7 * channels, cells), BF16)],
        compiler_params=pltpu.CompilerParams(vmem_limit_bytes=40 * 2**20),
    )(
        near_fine,
        table,
        full_fine.transpose(1, 0, 2).reshape(channels, 7 * channels),
        biases[0][:, None],
        pool,
    )

    every_octant = lax.all_gather(octants, "blocks", axis=0, tiled=True)
    parent = (first - 4) // 8

    def owner_of(block):
        below = starts[None, :] <= block[:, None]
        return (
            jnp.sum(below.astype(jnp.int32), axis=1) - 1,
            jnp.max(jnp.where(below, starts[None, :], 0), axis=1),
        )

    octant_ids = (parent - 2) * 8 + jnp.arange(64, dtype=jnp.int32)
    safe = jnp.clip(octant_ids, 0, total - 1)
    owner, start = owner_of(safe)
    octant_at = owner * slots + safe - start
    coarse_ids = parent - 1 + jnp.arange(6, dtype=jnp.int32)
    safe = jnp.clip(coarse_ids, 0, coarse_total - 1)
    owner, start = owner_of(safe * 8)
    cotangent_at = owner * coarse_slots + safe - (start + 7) // 8

    facts = jnp.stack(
        [
            chan,
            live,
            first - 4 - parent * 8,
            coarse_first - parent + 1,
            coarse_count,
            2 - parent,
            coarse_total - parent + 2,
        ]
    ).astype(jnp.int32)
    back_coarse = paired(full_coarse).transpose(2, 0, 1).reshape(channels, 7 * channels)
    back_fine = paired(full_fine).transpose(2, 0, 1).reshape(channels, 7 * channels)
    back_fine = lax.dynamic_slice_in_dim(back_fine, chan * group, group, 0)
    coarse_out, fine_grad, fine_wg, fine_bg, coarse_wg, coarse_bg = pl.pallas_call(
        backward_kernel,
        out_shape=(
            jax.ShapeDtypeStruct((coarse_slots, group, cells), BF16),
            jax.ShapeDtypeStruct((slots, group, cells), BF16),
            jax.ShapeDtypeStruct((7 * group, channels), F32),
            jax.ShapeDtypeStruct((group, channels), F32),
            jax.ShapeDtypeStruct((7 * group, channels), F32),
            jax.ShapeDtypeStruct((group, channels), F32),
        ),
        in_specs=[smem] * 4 + [vmem] * 10,
        out_specs=(vmem,) * 6,
        scratch_shapes=[
            pltpu.VMEM((7 * channels, cells), BF16),
            pltpu.VMEM((8, channels, cells), BF16),
            pltpu.VMEM((6, channels, cells), BF16),
            pltpu.VMEM((6, channels, cells), BF16),
            pltpu.VMEM((4, channels, cells), BF16),
            pltpu.VMEM((delta_rows + 1, channels, cells), BF16),
            pltpu.VMEM((group, cells), F32),
        ],
        compiler_params=pltpu.CompilerParams(vmem_limit_bytes=56 * 2**20),
    )(
        near_delta,
        facts,
        octant_at,
        cotangent_at,
        table,
        slope,
        every_octant,
        cotangents,
        full_coarse.transpose(1, 0, 2).reshape(channels, 7 * channels),
        biases[1][:, None],
        back_coarse,
        back_fine,
        place,
        spread,
    )
    partial = jnp.concatenate([fine_wg, fine_bg, coarse_wg, coarse_bg], axis=0)
    sums = jnp.sum(lax.all_gather(partial, "blocks", axis=0), axis=0)
    half = 8 * group
    fine_norm = jnp.sqrt(total.astype(F32) * cells)
    coarse_norm = jnp.sqrt(coarse_total.astype(F32) * cells)
    fine_sums = sums[:half] / fine_norm
    coarse_sums = sums[half:] / coarse_norm

    def weight_part(part):
        return paired(part[: 7 * group].reshape(7, group, channels))

    return (
        coarse_out,
        fine_grad,
        weight_part(fine_sums),
        fine_sums[7 * group :, 0],
        weight_part(coarse_sums),
        coarse_sums[7 * group :, 0],
    )


def solution(mesh):
    placed = (
        P("blocks", "chan", None),
        P(),
        P(None, "chan", None),
        P("chan"),
        P(None, "chan", None),
        P("chan"),
        P("blocks", "chan", None),
    )
    return jax.shard_map(
        local,
        mesh=mesh,
        in_specs=placed,
        out_specs=(
            P("blocks", "chan", None),
            P("blocks", "chan", None),
            P(None, "chan", None),
            P("chan"),
            P(None, "chan", None),
            P("chan"),
        ),
        check_vma=False,
    )
```

```python
import jax
import jax.numpy as jnp
import numpy as np
from jax import lax
from jax.experimental import pallas as pl
from jax.experimental.pallas import tpu as pltpu
from jax.sharding import PartitionSpec as P

EDGE = 8
CELLS = EDGE**3
TAP_PAIRS = (0, 2, 1, 4, 3, 6, 5)
STRIDES = (1, 8, 64)
F32 = jnp.float32
BF16 = jnp.bfloat16


def from_behind(block, axis, distance):
    devices = range(lax.axis_size(axis))
    route = [(i - distance, i) for i in devices if i - distance in devices]
    return lax.ppermute(block, axis, route)


def octant_maps():
    z, y, x = np.meshgrid(*[np.arange(EDGE)] * 3, indexing="ij")
    spread = np.zeros((8, CELLS, CELLS), np.float32)
    pool = np.zeros((2, CELLS, 128), np.float32)
    place = np.zeros((2, 8, 128, CELLS), np.float32)
    fine = np.arange(CELLS)
    small = ((z // 2) * 16 + (y // 2) * 4 + x // 2).reshape(-1)
    for half in range(2):
        pool[half, fine, small + 64 * half] = 1.0
    for q in range(8):
        cz, cy, cx = z // 2 + 4 * (q // 4), y // 2 + 4 * (q // 2 % 2), x // 2 + 4 * (q % 2)
        coarse = (cz * 64 + cy * 8 + cx).reshape(-1)
        spread[q, coarse, fine] = 1.0
        for half in range(2):
            place[half, q, small + 64 * half, coarse] = 1.0
    return spread, pool, place


def paired(taps):
    return jnp.stack([taps[t] for t in TAP_PAIRS])


def sigmoid(v):
    return 1.0 / (1.0 + jnp.exp(-v))


def write_views(views, own, neighbours, width):
    lane = lax.broadcasted_iota(jnp.int32, own.shape, 1)
    views[0:width, :] = own
    wide = own.astype(F32)
    for axis in range(3):
        stride = STRIDES[axis]
        coord = lane // stride % EDGE
        for side in range(2):
            near, far = (0, EDGE - 1) if side == 0 else (EDGE - 1, 0)
            step = stride if side == 0 else CELLS - stride
            wrap = (CELLS - 7 * stride) if side == 0 else 7 * stride
            tap = 1 + 2 * axis + side
            other = neighbours[2 * axis + side]
            if other is None:
                out = jnp.where(coord == near, 0.0, pltpu.roll(wide, step, 1))
            else:
                mixed = jnp.where(coord == far, other.astype(F32), wide)
                out = pltpu.roll(mixed, step, 1)
                if step != wrap % CELLS:
                    out = jnp.where(coord == near, pltpu.roll(mixed, wrap, 1), out)
            views[tap * width : (tap + 1) * width, :] = out.astype(BF16)


def forward_kernel(near, table, weight, bias, pool, slope, octants, views):
    width = table.shape[1]

    def row(j, carry):
        own = table[j + 4]
        write_views(views, own, [table[near[j * 6 + n]] for n in range(6)], width)
        v = jnp.dot(weight[...], views[...], preferred_element_type=F32) + bias[...]
        s = sigmoid(v)
        slope[j] = s * (1.0 + v * (1.0 - s))

        @pl.when(jnp.logical_and(j >= 4, j < 20))
        def _():
            hidden = (v * s).astype(BF16)
            half = j % 2
            small = jnp.dot(hidden, pool[half], preferred_element_type=F32) * 0.125
            pair = (j - 4) // 2
            kept = jnp.where(half == 0, 0.0, octants[pair].astype(F32))
            octants[pair] = (kept + small).astype(BF16)

        return carry

    lax.fori_loop(0, slope.shape[0], row, 0)


def backward_kernel(
    near, facts, octant_at, cotangent_at, table, slope, octants, cotangent, forward_w, coarse_b, back_coarse_w, back_w,
    place, spread,
    coarse_out, fine_grad, fine_wg, fine_bg, coarse_wg, coarse_bg,
    views, coarse_in, coarse_act, coarse_delta, coarse_back, fine_delta, bias_sum,
):
    width = table.shape[1]
    slots, group = fine_grad.shape[0], fine_grad.shape[1]
    chan, live, parent0, coarse_row, coarse_live = (facts[n] for n in range(5))
    mine = pl.ds(pl.multiple_of(chan * group, group), group)

    def own_views():
        return jnp.concatenate(
            [views[pl.ds(pl.multiple_of(t * width + chan * group, group), group), :] for t in range(7)],
            axis=0,
        )

    def assemble(k, carry):
        total = jnp.zeros((width, CELLS), F32)
        for q in range(8):
            at = octant_at[k * 8 + q]
            owner, slot = at // slots, at % slots
            both = jnp.concatenate(
                [octants[c, owner, slot // 2] for c in range(octants.shape[0])], axis=0
            )
            total += jnp.dot(both, place[slot % 2, q], preferred_element_type=F32)
        inside = jnp.logical_and(k >= facts[5], k < facts[6])
        coarse_in[k] = jnp.where(inside, total, 0.0).astype(BF16)
        return carry

    lax.fori_loop(0, 8, assemble, 0)

    def coarse_forward(k, carry):
        write_views(
            views, coarse_in[k + 1], [None] * 4 + [coarse_in[k], coarse_in[k + 2]], width
        )
        v = jnp.dot(forward_w[...], views[...], preferred_element_type=F32) + coarse_b[...]
        s = sigmoid(v)
        coarse_act[k] = (v * s).astype(BF16)
        inside = jnp.logical_and(k + 1 >= facts[5], k + 1 < facts[6])
        delta = cotangent[cotangent_at[k]].astype(F32) * (s * (1.0 + v * (1.0 - s)))
        coarse_delta[k] = jnp.where(inside, delta, 0.0).astype(BF16)
        return carry

    lax.fori_loop(0, 6, coarse_forward, 0)
    for s in range(coarse_out.shape[0]):
        row = jnp.minimum(coarse_row + s, 5)
        kept = jnp.where(s < coarse_live, coarse_act[row, mine, :].astype(F32), 0.0)
        coarse_out[s] = kept.astype(BF16)

    coarse_wg[...] = jnp.zeros_like(coarse_wg)
    bias_sum[...] = jnp.zeros_like(bias_sum)

    def coarse_backward(k, carry):
        write_views(
            views,
            coarse_delta[k + 1],
            [None] * 4 + [coarse_delta[k], coarse_delta[k + 2]],
            width,
        )
        coarse_back[k] = jnp.dot(
            back_coarse_w[...], views[...], preferred_element_type=F32
        ).astype(BF16)
        row = k + 1

        @pl.when(jnp.logical_and(row >= coarse_row, row < coarse_row + coarse_live))
        def _():
            coarse_wg[...] += lax.dot_general(
                own_views(), coarse_in[k + 2], (((1,), (1,)), ((), ())), preferred_element_type=F32
            )
            bias_sum[...] += coarse_delta[row, mine, :].astype(F32)

        return carry

    lax.fori_loop(0, 4, coarse_backward, 0)
    coarse_bg[...] = jnp.broadcast_to(
        jnp.sum(bias_sum[...], axis=1, keepdims=True), coarse_bg.shape
    )

    def delta_row(j, carry):
        index = parent0 + j
        up = jnp.dot(coarse_back[index // 8], spread[index % 8], preferred_element_type=F32)
        fine_delta[j] = (up * 0.125 * slope[j]).astype(BF16)
        return carry

    lax.fori_loop(0, slope.shape[0], delta_row, 0)
    fine_delta[slope.shape[0]] = jnp.zeros((width, CELLS), BF16)
    fine_wg[...] = jnp.zeros_like(fine_wg)
    bias_sum[...] = jnp.zeros_like(bias_sum)

    def fine_row(r, carry):
        @pl.when(r < live)
        def _():
            write_views(
                views, fine_delta[r + 4], [fine_delta[near[r * 6 + n]] for n in range(6)], width
            )
            fine_grad[r] = jnp.dot(back_w[...], views[...], preferred_element_type=F32).astype(BF16)
            fine_wg[...] += lax.dot_general(
                own_views(), table[r + 8], (((1,), (1,)), ((), ())), preferred_element_type=F32
            )
            bias_sum[...] += fine_delta[r + 4, mine, :].astype(F32)

        @pl.when(r >= live)
        def _():
            fine_grad[r] = jnp.zeros((group, CELLS), BF16)

        return carry

    lax.fori_loop(0, fine_grad.shape[0], fine_row, 0)
    fine_bg[...] = jnp.broadcast_to(jnp.sum(bias_sum[...], axis=1, keepdims=True), fine_bg.shape)


def greet(axis):
    size, me = lax.axis_size(axis), lax.axis_index(axis)
    barrier = pltpu.get_barrier_semaphore()

    def one(d, carry):
        pl.semaphore_signal(
            barrier, inc=1, device_id={axis: (me + d) % size}, device_id_type=pl.DeviceIdType.MESH
        )
        return carry

    lax.fori_loop(1, size, one, 0)
    return size - 1


def push(src, dst, send_sem, recv_sem, axis, peer):
    return pltpu.make_async_remote_copy(
        src_ref=src,
        dst_ref=dst,
        send_sem=send_sem,
        recv_sem=recv_sem,
        device_id={axis: peer},
        device_id_type=pl.DeviceIdType.MESH,
    )


def exchange(axis, source, target, send_sem, recv_sem):
    size, me = lax.axis_size(axis), lax.axis_index(axis)

    def start(d, carry):
        peer = (me + d) % size
        push(source(peer), target(me, d), send_sem.at[d], recv_sem.at[d], axis, peer).start()
        return carry

    def finish(d, carry):
        peer = (me + d) % size
        giver = (me + size - d) % size
        push(source(peer), target(me, d), send_sem.at[d], recv_sem.at[d], axis, peer).wait_send()
        push(source(peer), target(giver, d), send_sem.at[d], recv_sem.at[d], axis, peer).wait_recv()
        return carry

    lax.fori_loop(1, size, start, 0)
    lax.fori_loop(1, size, finish, 0)


def octant_kernel(octants, out, send_b, recv_b, send_c, recv_c, own_sem):
    me, chan = lax.axis_index("blocks"), lax.axis_index("chan")
    group = out.shape[3]
    pl.semaphore_wait(pltpu.get_barrier_semaphore(), greet("blocks") + greet("chan"))
    mine = octants.at[:, pl.ds(pl.multiple_of(chan * group, group), group), :]
    kept = pltpu.make_async_copy(mine, out.at[chan, me], own_sem)
    kept.start()
    exchange("blocks", lambda p: mine, lambda p, d: out.at[chan, p], send_b, recv_b)
    kept.wait()
    exchange("chan", lambda p: out.at[chan], lambda p, d: out.at[p], send_c, recv_c)


def share_octants(octants, group):
    n, width = lax.axis_size("blocks"), lax.axis_size("chan")
    return pl.pallas_call(
        octant_kernel,
        out_shape=jax.ShapeDtypeStruct((width, n, octants.shape[0], group, 128), BF16),
        in_specs=[pl.BlockSpec(memory_space=pltpu.VMEM)],
        out_specs=pl.BlockSpec(memory_space=pltpu.VMEM),
        scratch_shapes=[
            pltpu.SemaphoreType.DMA((n,)),
            pltpu.SemaphoreType.DMA((n,)),
            pltpu.SemaphoreType.DMA((width,)),
            pltpu.SemaphoreType.DMA((width,)),
            pltpu.SemaphoreType.DMA,
        ],
        compiler_params=pltpu.CompilerParams(
            collective_id=1, has_side_effects=True, vmem_limit_bytes=32 * 2**20
        ),
    )(octants)


def sum_kernel(part, out, landed, send_a, recv_a, send_b, recv_b):
    me = lax.axis_index("blocks")
    size = part.shape[0]
    pl.semaphore_wait(pltpu.get_barrier_semaphore(), greet("blocks"))
    exchange("blocks", lambda p: part.at[p], lambda p, d: landed.at[d], send_a, recv_a)
    out[me] = lax.fori_loop(1, size, lambda d, total: total + landed[d], part[me])
    exchange("blocks", lambda p: out.at[me], lambda p, d: out.at[p], send_b, recv_b)


def sum_over_blocks(partial):
    n = lax.axis_size("blocks")
    rows, width = partial.shape
    shape = (n, rows // n, width)
    summed = pl.pallas_call(
        sum_kernel,
        out_shape=jax.ShapeDtypeStruct(shape, F32),
        in_specs=[pl.BlockSpec(memory_space=pltpu.VMEM)],
        out_specs=pl.BlockSpec(memory_space=pltpu.VMEM),
        scratch_shapes=[pltpu.VMEM(shape, F32)] + [pltpu.SemaphoreType.DMA((n,))] * 4,
        compiler_params=pltpu.CompilerParams(collective_id=2, has_side_effects=True),
    )(partial.reshape(shape))
    return summed.reshape(rows, width)


def local(
    fine_input, block_counts, fine_weight, fine_bias, coarse_weight, coarse_bias, coarse_cotangent
):
    slots, group, cells = fine_input.shape
    coarse_slots = coarse_cotangent.shape[0]
    channels = fine_weight.shape[2]
    device = lax.axis_index("blocks")
    chan = lax.axis_index("chan")
    order = jnp.arange(block_counts.shape[0])
    earlier = order[None, :] < order[:, None]
    starts = jnp.sum(jnp.where(earlier, block_counts[None, :], 0), axis=1)
    first = starts[device]
    live = block_counts[device]
    total = jnp.sum(block_counts)
    coarse_total = total // 8
    coarse_first = (first + 7) // 8
    coarse_count = (first + live + 7) // 8 - coarse_first

    lower = from_behind(lax.dynamic_slice_in_dim(fine_input, live - 8, 8, 0), "blocks", 1)
    upper = from_behind(fine_input[:8], "blocks", -1)
    rows = slots + 16
    table = jnp.concatenate([lower, fine_input, jnp.zeros((9, group, cells), BF16)], axis=0)
    table = lax.dynamic_update_slice_in_dim(table, upper, 8 + live, 0)
    table = lax.all_gather(table, "chan", axis=1, tiled=True)
    weights = lax.all_gather(
        jnp.concatenate([fine_weight, coarse_weight]), "chan", axis=1, tiled=True
    )
    biases = lax.all_gather(jnp.stack([fine_bias, coarse_bias]), "chan", axis=1, tiled=True)
    cotangents = lax.all_gather(
        lax.all_gather(coarse_cotangent, "chan", axis=1, tiled=True), "blocks", axis=0, tiled=True
    )
    full_fine, full_coarse = weights[:7], weights[7:]

    spread, pool, place = (jnp.asarray(a, BF16) for a in octant_maps())
    delta_rows = slots + 8
    ids = first - 4 + jnp.arange(delta_rows, dtype=jnp.int32)
    px, py = ids % 2, ids // 2 % 2
    valid = jnp.stack(
        [px == 1, px == 0, py == 1, py == 0, ids >= 4, ids + 4 < total], axis=1
    )
    offsets = jnp.array([-1, 1, -2, 2, -4, 4], jnp.int32)[None, :]
    spot = jnp.arange(delta_rows, dtype=jnp.int32)[:, None] + offsets
    near_fine = jnp.where(valid, spot + 4, rows).reshape(-1)
    near_delta = jnp.where(valid, spot, delta_rows)[4 : 4 + slots].reshape(-1)

    smem = pl.BlockSpec(memory_space=pltpu.SMEM)
    vmem = pl.BlockSpec(memory_space=pltpu.VMEM)
    slope, octants = pl.pallas_call(
        forward_kernel,
        out_shape=(
            jax.ShapeDtypeStruct((delta_rows, channels, cells), F32),
            jax.ShapeDtypeStruct((slots // 2, channels, 128), BF16),
        ),
        in_specs=[smem] + [vmem] * 4,
        out_specs=(vmem, vmem),
        scratch_shapes=[pltpu.VMEM((7 * channels, cells), BF16)],
        compiler_params=pltpu.CompilerParams(vmem_limit_bytes=40 * 2**20),
    )(
        near_fine,
        table,
        full_fine.transpose(1, 0, 2).reshape(channels, 7 * channels),
        biases[0][:, None],
        pool,
    )

    every_octant = share_octants(octants, group)
    parent = (first - 4) // 8

    def owner_of(block):
        below = starts[None, :] <= block[:, None]
        return (
            jnp.sum(below.astype(jnp.int32), axis=1) - 1,
            jnp.max(jnp.where(below, starts[None, :], 0), axis=1),
        )

    octant_ids = (parent - 2) * 8 + jnp.arange(64, dtype=jnp.int32)
    safe = jnp.clip(octant_ids, 0, total - 1)
    owner, start = owner_of(safe)
    octant_at = owner * slots + safe - start
    coarse_ids = parent - 1 + jnp.arange(6, dtype=jnp.int32)
    safe = jnp.clip(coarse_ids, 0, coarse_total - 1)
    owner, start = owner_of(safe * 8)
    cotangent_at = owner * coarse_slots + safe - (start + 7) // 8

    facts = jnp.stack(
        [
            chan,
            live,
            first - 4 - parent * 8,
            coarse_first - parent + 1,
            coarse_count,
            2 - parent,
            coarse_total - parent + 2,
        ]
    ).astype(jnp.int32)
    back_coarse = paired(full_coarse).transpose(2, 0, 1).reshape(channels, 7 * channels)
    back_fine = paired(full_fine).transpose(2, 0, 1).reshape(channels, 7 * channels)
    back_fine = lax.dynamic_slice_in_dim(back_fine, chan * group, group, 0)
    coarse_out, fine_grad, fine_wg, fine_bg, coarse_wg, coarse_bg = pl.pallas_call(
        backward_kernel,
        out_shape=(
            jax.ShapeDtypeStruct((coarse_slots, group, cells), BF16),
            jax.ShapeDtypeStruct((slots, group, cells), BF16),
            jax.ShapeDtypeStruct((7 * group, channels), F32),
            jax.ShapeDtypeStruct((group, channels), F32),
            jax.ShapeDtypeStruct((7 * group, channels), F32),
            jax.ShapeDtypeStruct((group, channels), F32),
        ),
        in_specs=[smem] * 4 + [vmem] * 10,
        out_specs=(vmem,) * 6,
        scratch_shapes=[
            pltpu.VMEM((7 * channels, cells), BF16),
            pltpu.VMEM((8, channels, cells), BF16),
            pltpu.VMEM((6, channels, cells), BF16),
            pltpu.VMEM((6, channels, cells), BF16),
            pltpu.VMEM((4, channels, cells), BF16),
            pltpu.VMEM((delta_rows + 1, channels, cells), BF16),
            pltpu.VMEM((group, cells), F32),
        ],
        compiler_params=pltpu.CompilerParams(vmem_limit_bytes=56 * 2**20),
    )(
        near_delta,
        facts,
        octant_at,
        cotangent_at,
        table,
        slope,
        every_octant,
        cotangents,
        full_coarse.transpose(1, 0, 2).reshape(channels, 7 * channels),
        biases[1][:, None],
        back_coarse,
        back_fine,
        place,
        spread,
    )
    partial = jnp.concatenate([fine_wg, fine_bg, coarse_wg, coarse_bg], axis=0)
    sums = sum_over_blocks(partial)
    half = 8 * group
    fine_norm = jnp.sqrt(total.astype(F32) * cells)
    coarse_norm = jnp.sqrt(coarse_total.astype(F32) * cells)
    fine_sums = sums[:half] / fine_norm
    coarse_sums = sums[half:] / coarse_norm

    def weight_part(part):
        return paired(part[: 7 * group].reshape(7, group, channels))

    return (
        coarse_out,
        fine_grad,
        weight_part(fine_sums),
        fine_sums[7 * group :, 0],
        weight_part(coarse_sums),
        coarse_sums[7 * group :, 0],
    )


def solution(mesh):
    placed = (
        P("blocks", "chan", None),
        P(),
        P(None, "chan", None),
        P("chan"),
        P(None, "chan", None),
        P("chan"),
        P("blocks", "chan", None),
    )
    return jax.shard_map(
        local,
        mesh=mesh,
        in_specs=placed,
        out_specs=(
            P("blocks", "chan", None),
            P("blocks", "chan", None),
            P(None, "chan", None),
            P("chan"),
            P(None, "chan", None),
            P("chan"),
        ),
        check_vma=False,
    )
```

```python
import jax
import jax.numpy as jnp
import numpy as np
from jax import lax
from jax.experimental import pallas as pl
from jax.experimental.pallas import tpu as pltpu
from jax.sharding import PartitionSpec as P

EDGE = 8
CELLS = EDGE**3
TAP_PAIRS = (0, 2, 1, 4, 3, 6, 5)
STRIDES = (1, 8, 64)
F32 = jnp.float32
BF16 = jnp.bfloat16


def octant_maps():
    z, y, x = np.meshgrid(*[np.arange(EDGE)] * 3, indexing="ij")
    spread = np.zeros((8, CELLS, CELLS), np.float32)
    pool = np.zeros((2, CELLS, 128), np.float32)
    place = np.zeros((2, 8, 128, CELLS), np.float32)
    fine = np.arange(CELLS)
    small = ((z // 2) * 16 + (y // 2) * 4 + x // 2).reshape(-1)
    for half in range(2):
        pool[half, fine, small + 64 * half] = 1.0
    for q in range(8):
        cz, cy, cx = z // 2 + 4 * (q // 4), y // 2 + 4 * (q // 2 % 2), x // 2 + 4 * (q % 2)
        coarse = (cz * 64 + cy * 8 + cx).reshape(-1)
        spread[q, coarse, fine] = 1.0
        for half in range(2):
            place[half, q, small + 64 * half, coarse] = 1.0
    return spread, pool, place


def paired(taps):
    return jnp.stack([taps[t] for t in TAP_PAIRS])


def sigmoid(v):
    return 1.0 / (1.0 + jnp.exp(-v))


def write_views(views, own, neighbours, width):
    lane = lax.broadcasted_iota(jnp.int32, own.shape, 1)
    views[0:width, :] = own
    wide = own.astype(F32)
    for axis in range(3):
        stride = STRIDES[axis]
        coord = lane // stride % EDGE
        for side in range(2):
            near, far = (0, EDGE - 1) if side == 0 else (EDGE - 1, 0)
            step = stride if side == 0 else CELLS - stride
            wrap = (CELLS - 7 * stride) if side == 0 else 7 * stride
            tap = 1 + 2 * axis + side
            other = neighbours[2 * axis + side]
            if other is None:
                out = jnp.where(coord == near, 0.0, pltpu.roll(wide, step, 1))
            else:
                mixed = jnp.where(coord == far, other.astype(F32), wide)
                out = pltpu.roll(mixed, step, 1)
                if step != wrap % CELLS:
                    out = jnp.where(coord == near, pltpu.roll(mixed, wrap, 1), out)
            views[tap * width : (tap + 1) * width, :] = out.astype(BF16)


def forward_kernel(near, table, weight, bias, pool, slope, octants, views):
    width = table.shape[1]

    def row(j, carry):
        own = table[near[j * 7 + 6]]
        write_views(views, own, [table[near[j * 7 + n]] for n in range(6)], width)
        v = jnp.dot(weight[...], views[...], preferred_element_type=F32) + bias[...]
        s = sigmoid(v)
        slope[j] = s * (1.0 + v * (1.0 - s))

        @pl.when(jnp.logical_and(j >= 4, j < 20))
        def _():
            hidden = (v * s).astype(BF16)
            half = j % 2
            small = jnp.dot(hidden, pool[half], preferred_element_type=F32) * 0.125
            pair = (j - 4) // 2
            kept = jnp.where(half == 0, 0.0, octants[pair].astype(F32))
            octants[pair] = (kept + small).astype(BF16)

        return carry

    lax.fori_loop(0, slope.shape[0], row, 0)


def backward_kernel(
    near, facts, octant_at, cotangent_at, table, slope, octants, cotangent, forward_w, coarse_b, back_coarse_w, back_w,
    place, spread,
    coarse_out, fine_grad, fine_wg, fine_bg, coarse_wg, coarse_bg,
    views, coarse_in, coarse_act, coarse_delta, coarse_back, fine_delta, bias_sum,
):
    width = table.shape[1]
    slots, group = fine_grad.shape[0], fine_grad.shape[1]
    chan, live, parent0, coarse_row, coarse_live = (facts[n] for n in range(5))
    mine = pl.ds(pl.multiple_of(chan * group, group), group)

    def own_views():
        return jnp.concatenate(
            [views[pl.ds(pl.multiple_of(t * width + chan * group, group), group), :] for t in range(7)],
            axis=0,
        )

    def assemble(k, carry):
        total = jnp.zeros((width, CELLS), F32)
        for q in range(8):
            at = octant_at[k * 8 + q]
            owner, slot = at // slots, at % slots
            both = jnp.concatenate(
                [octants[c, owner, slot // 2] for c in range(octants.shape[0])], axis=0
            )
            total += jnp.dot(both, place[slot % 2, q], preferred_element_type=F32)
        inside = jnp.logical_and(k >= facts[5], k < facts[6])
        coarse_in[k] = jnp.where(inside, total, 0.0).astype(BF16)
        return carry

    lax.fori_loop(0, 8, assemble, 0)

    def coarse_forward(k, carry):
        write_views(
            views, coarse_in[k + 1], [None] * 4 + [coarse_in[k], coarse_in[k + 2]], width
        )
        v = jnp.dot(forward_w[...], views[...], preferred_element_type=F32) + coarse_b[...]
        s = sigmoid(v)
        coarse_act[k] = (v * s).astype(BF16)
        inside = jnp.logical_and(k + 1 >= facts[5], k + 1 < facts[6])
        delta = cotangent[cotangent_at[k]].astype(F32) * (s * (1.0 + v * (1.0 - s)))
        coarse_delta[k] = jnp.where(inside, delta, 0.0).astype(BF16)
        return carry

    lax.fori_loop(0, 6, coarse_forward, 0)
    for s in range(coarse_out.shape[0]):
        row = jnp.minimum(coarse_row + s, 5)
        kept = jnp.where(s < coarse_live, coarse_act[row, mine, :].astype(F32), 0.0)
        coarse_out[s] = kept.astype(BF16)

    coarse_wg[...] = jnp.zeros_like(coarse_wg)
    bias_sum[...] = jnp.zeros_like(bias_sum)

    def coarse_backward(k, carry):
        write_views(
            views,
            coarse_delta[k + 1],
            [None] * 4 + [coarse_delta[k], coarse_delta[k + 2]],
            width,
        )
        coarse_back[k] = jnp.dot(
            back_coarse_w[...], views[...], preferred_element_type=F32
        ).astype(BF16)
        row = k + 1

        @pl.when(jnp.logical_and(row >= coarse_row, row < coarse_row + coarse_live))
        def _():
            coarse_wg[...] += lax.dot_general(
                own_views(), coarse_in[k + 2], (((1,), (1,)), ((), ())), preferred_element_type=F32
            )
            bias_sum[...] += coarse_delta[row, mine, :].astype(F32)

        return carry

    lax.fori_loop(0, 4, coarse_backward, 0)
    coarse_bg[...] = jnp.broadcast_to(
        jnp.sum(bias_sum[...], axis=1, keepdims=True), coarse_bg.shape
    )

    def delta_row(j, carry):
        index = parent0 + j
        up = jnp.dot(coarse_back[index // 8], spread[index % 8], preferred_element_type=F32)
        fine_delta[j] = (up * 0.125 * slope[j]).astype(BF16)
        return carry

    lax.fori_loop(0, slope.shape[0], delta_row, 0)
    fine_delta[slope.shape[0]] = jnp.zeros((width, CELLS), BF16)
    fine_wg[...] = jnp.zeros_like(fine_wg)
    bias_sum[...] = jnp.zeros_like(bias_sum)

    def fine_row(r, carry):
        @pl.when(r < live)
        def _():
            write_views(
                views, fine_delta[r + 4], [fine_delta[near[r * 6 + n]] for n in range(6)], width
            )
            fine_grad[r] = jnp.dot(back_w[...], views[...], preferred_element_type=F32).astype(BF16)
            fine_wg[...] += lax.dot_general(
                own_views(), table[r + 8], (((1,), (1,)), ((), ())), preferred_element_type=F32
            )
            bias_sum[...] += fine_delta[r + 4, mine, :].astype(F32)

        @pl.when(r >= live)
        def _():
            fine_grad[r] = jnp.zeros((group, CELLS), BF16)

        return carry

    lax.fori_loop(0, fine_grad.shape[0], fine_row, 0)
    fine_bg[...] = jnp.broadcast_to(jnp.sum(bias_sum[...], axis=1, keepdims=True), fine_bg.shape)


def greet(axis):
    size, me = lax.axis_size(axis), lax.axis_index(axis)
    barrier = pltpu.get_barrier_semaphore()

    def one(d, carry):
        pl.semaphore_signal(
            barrier, inc=1, device_id={axis: (me + d) % size}, device_id_type=pl.DeviceIdType.MESH
        )
        return carry

    lax.fori_loop(1, size, one, 0)
    return size - 1


def push(src, dst, send_sem, recv_sem, axis, peer):
    return pltpu.make_async_remote_copy(
        src_ref=src,
        dst_ref=dst,
        send_sem=send_sem,
        recv_sem=recv_sem,
        device_id={axis: peer},
        device_id_type=pl.DeviceIdType.MESH,
    )


def exchange(axis, source, target, send_sem, recv_sem):
    size, me = lax.axis_size(axis), lax.axis_index(axis)

    def start(d, carry):
        peer = (me + d) % size
        push(source(peer), target(me, d), send_sem.at[d], recv_sem.at[d], axis, peer).start()
        return carry

    def finish(d, carry):
        peer = (me + d) % size
        giver = (me + size - d) % size
        push(source(peer), target(me, d), send_sem.at[d], recv_sem.at[d], axis, peer).wait_send()
        push(source(peer), target(giver, d), send_sem.at[d], recv_sem.at[d], axis, peer).wait_recv()
        return carry

    lax.fori_loop(1, size, start, 0)
    lax.fori_loop(1, size, finish, 0)


def chan_peers():
    me = lax.axis_index("chan")
    size = lax.axis_size("chan")
    far, near = (me + size // 2) % size, me + 1 - 2 * (me % 2)
    return me, far, near, (near + size // 2) % size


def greet_chan():
    _, far, near, _ = chan_peers()
    for peer in (far, near):
        pl.semaphore_signal(
            pltpu.get_barrier_semaphore(),
            inc=1,
            device_id={"chan": peer},
            device_id_type=pl.DeviceIdType.MESH,
        )
    return 2


def share_chan(parts, send_sem, recv_sem, base):
    me, far, near, near_far = chan_peers()

    def copy(n, k, held, peer):
        place = parts[n](held)
        at = base + 3 * n + k
        return push(place, place, send_sem.at[at], recv_sem.at[at], "chan", peer)

    def first():
        for n in range(len(parts)):
            copy(n, 0, me, far).start()
            copy(n, 1, me, near).start()

    def second():
        for n in range(len(parts)):
            copy(n, 0, far, far).wait_recv()
            copy(n, 2, far, near).start()
        return third

    def third():
        for n in range(len(parts)):
            copy(n, 1, near, near).wait_recv()
            copy(n, 2, near_far, near).wait_recv()
            copy(n, 0, me, far).wait_send()
            copy(n, 1, me, near).wait_send()
            copy(n, 2, far, near).wait_send()

    return first, second


def gather_kernel(
    tail, own, weight, bias, cotangent, table, weights, biases, cotangents,
    send_b, recv_b, send_c, recv_c,
):
    me, n = lax.axis_index("blocks"), lax.axis_size("blocks")
    chan = lax.axis_index("chan")
    slots, group, cells = own.shape
    after, before = (me + 1) % n, (me + n - 1) % n
    for peer in (after, before):
        pl.semaphore_signal(
            pltpu.get_barrier_semaphore(),
            inc=1,
            device_id={"blocks": peer},
            device_id_type=pl.DeviceIdType.MESH,
        )
    pl.semaphore_wait(pltpu.get_barrier_semaphore(), greet_chan() + 2)

    def lane(c):
        return pl.ds(pl.multiple_of(c * group, group), group)

    def rows(first, count):
        return lambda c: table.at[pl.ds(first, count), lane(c), :]

    lower, upper = rows(0, 8), rows(8 + slots, 8)
    down = push(own.at[pl.ds(0, 8)], upper(chan), send_b.at[0], recv_b.at[0], "blocks", before)
    up = push(tail, lower(chan), send_b.at[1], recv_b.at[1], "blocks", after)
    down.start()
    up.start()
    table[8 : 8 + slots, lane(chan), :] = own[...]
    weights[:, lane(chan), :] = weight[...]
    biases[chan] = bias[...]
    cotangents[:, lane(chan), :] = cotangent[...]
    table[16 + slots] = jnp.zeros(table.shape[1:], BF16)
    first, second = share_chan(
        [
            rows(8, slots),
            lambda c: weights.at[:, lane(c), :],
            lambda c: biases.at[c],
            lambda c: cotangents.at[:, lane(c), :],
        ],
        send_c, recv_c, 0,
    )
    halo_first, halo_second = share_chan([lower, upper], send_c, recv_c, 12)
    first()
    down.wait()
    up.wait()
    halo_first()
    third = second()
    halo_third = halo_second()
    third()
    halo_third()


def gather_start(tail, own, weight, bias, cotangent):
    width = lax.axis_size("chan")
    slots, group, cells = own.shape
    channels = group * width
    vmem = pl.BlockSpec(memory_space=pltpu.VMEM)
    return pl.pallas_call(
        gather_kernel,
        out_shape=(
            jax.ShapeDtypeStruct((slots + 17, channels, cells), BF16),
            jax.ShapeDtypeStruct((weight.shape[0], channels, channels), BF16),
            jax.ShapeDtypeStruct((width,) + bias.shape, F32),
            jax.ShapeDtypeStruct((cotangent.shape[0], channels, cells), BF16),
        ),
        in_specs=[vmem] * 5,
        out_specs=(vmem,) * 4,
        scratch_shapes=[
            pltpu.SemaphoreType.DMA((2,)),
            pltpu.SemaphoreType.DMA((2,)),
            pltpu.SemaphoreType.DMA((18,)),
            pltpu.SemaphoreType.DMA((18,)),
        ],
        compiler_params=pltpu.CompilerParams(
            collective_id=3, has_side_effects=True, vmem_limit_bytes=32 * 2**20
        ),
    )(tail, own, weight, bias, cotangent)


def octant_kernel(octants, out, send_b, recv_b, send_c, recv_c, own_sem):
    me, chan = lax.axis_index("blocks"), lax.axis_index("chan")
    group = out.shape[3]
    pl.semaphore_wait(pltpu.get_barrier_semaphore(), greet("blocks") + greet_chan())
    mine = octants.at[:, pl.ds(pl.multiple_of(chan * group, group), group), :]
    kept = pltpu.make_async_copy(mine, out.at[chan, me], own_sem)
    kept.start()
    exchange("blocks", lambda p: mine, lambda p, d: out.at[chan, p], send_b, recv_b)
    kept.wait()
    first, second = share_chan([lambda c: out.at[c]], send_c, recv_c, 0)
    first()
    second()()


def share_octants(octants, group):
    n, width = lax.axis_size("blocks"), lax.axis_size("chan")
    return pl.pallas_call(
        octant_kernel,
        out_shape=jax.ShapeDtypeStruct((width, n, octants.shape[0], group, 128), BF16),
        in_specs=[pl.BlockSpec(memory_space=pltpu.VMEM)],
        out_specs=pl.BlockSpec(memory_space=pltpu.VMEM),
        scratch_shapes=[
            pltpu.SemaphoreType.DMA((n,)),
            pltpu.SemaphoreType.DMA((n,)),
            pltpu.SemaphoreType.DMA((3,)),
            pltpu.SemaphoreType.DMA((3,)),
            pltpu.SemaphoreType.DMA,
        ],
        compiler_params=pltpu.CompilerParams(
            collective_id=1, has_side_effects=True, vmem_limit_bytes=32 * 2**20
        ),
    )(octants)


def sum_kernel(part, out, landed, send_a, recv_a, send_b, recv_b):
    me = lax.axis_index("blocks")
    size = part.shape[0]
    pl.semaphore_wait(pltpu.get_barrier_semaphore(), greet("blocks"))
    exchange("blocks", lambda p: part.at[p], lambda p, d: landed.at[d], send_a, recv_a)
    out[me] = lax.fori_loop(1, size, lambda d, total: total + landed[d], part[me])
    exchange("blocks", lambda p: out.at[me], lambda p, d: out.at[p], send_b, recv_b)


def sum_over_blocks(partial):
    n = lax.axis_size("blocks")
    rows, width = partial.shape
    shape = (n, rows // n, width)
    summed = pl.pallas_call(
        sum_kernel,
        out_shape=jax.ShapeDtypeStruct(shape, F32),
        in_specs=[pl.BlockSpec(memory_space=pltpu.VMEM)],
        out_specs=pl.BlockSpec(memory_space=pltpu.VMEM),
        scratch_shapes=[pltpu.VMEM(shape, F32)] + [pltpu.SemaphoreType.DMA((n,))] * 4,
        compiler_params=pltpu.CompilerParams(collective_id=2, has_side_effects=True),
    )(partial.reshape(shape))
    return summed.reshape(rows, width)


def local(
    fine_input, block_counts, fine_weight, fine_bias, coarse_weight, coarse_bias, coarse_cotangent
):
    slots, group, cells = fine_input.shape
    coarse_slots = coarse_cotangent.shape[0]
    channels = fine_weight.shape[2]
    device = lax.axis_index("blocks")
    chan = lax.axis_index("chan")
    order = jnp.arange(block_counts.shape[0])
    earlier = order[None, :] < order[:, None]
    starts = jnp.sum(jnp.where(earlier, block_counts[None, :], 0), axis=1)
    first = starts[device]
    live = block_counts[device]
    total = jnp.sum(block_counts)
    coarse_total = total // 8
    coarse_first = (first + 7) // 8
    coarse_count = (first + live + 7) // 8 - coarse_first

    rows = slots + 16
    tail = lax.dynamic_slice_in_dim(fine_input, live - 8, 8, 0)
    table, weights, biases, cotangents = gather_start(
        tail,
        fine_input,
        jnp.concatenate([fine_weight, coarse_weight]),
        jnp.stack([fine_bias, coarse_bias]),
        coarse_cotangent,
    )
    biases = biases.transpose(1, 0, 2).reshape(2, channels)
    cotangents = lax.all_gather(cotangents, "blocks", axis=0, tiled=True)
    full_fine, full_coarse = weights[:7], weights[7:]

    spread, pool, place = (jnp.asarray(a, BF16) for a in octant_maps())
    delta_rows = slots + 8
    ids = first - 4 + jnp.arange(delta_rows, dtype=jnp.int32)
    px, py = ids % 2, ids // 2 % 2
    valid = jnp.stack(
        [px == 1, px == 0, py == 1, py == 0, ids >= 4, ids + 4 < total], axis=1
    )
    offsets = jnp.array([-1, 1, -2, 2, -4, 4], jnp.int32)[None, :]
    spot = jnp.arange(delta_rows, dtype=jnp.int32)[:, None] + offsets

    def table_row(r):
        return jnp.where(r < 8 + live, r, jnp.minimum(r + slots - live, rows - 1))

    own_row = table_row(jnp.arange(delta_rows, dtype=jnp.int32) + 4)
    near_fine = jnp.where(valid, table_row(spot + 4), rows)
    near_fine = jnp.concatenate([near_fine, own_row[:, None]], axis=1).reshape(-1)
    near_delta = jnp.where(valid, spot, delta_rows)[4 : 4 + slots].reshape(-1)

    smem = pl.BlockSpec(memory_space=pltpu.SMEM)
    vmem = pl.BlockSpec(memory_space=pltpu.VMEM)
    slope, octants = pl.pallas_call(
        forward_kernel,
        out_shape=(
            jax.ShapeDtypeStruct((delta_rows, channels, cells), F32),
            jax.ShapeDtypeStruct((slots // 2, channels, 128), BF16),
        ),
        in_specs=[smem] + [vmem] * 4,
        out_specs=(vmem, vmem),
        scratch_shapes=[pltpu.VMEM((7 * channels, cells), BF16)],
        compiler_params=pltpu.CompilerParams(vmem_limit_bytes=40 * 2**20),
    )(
        near_fine,
        table,
        full_fine.transpose(1, 0, 2).reshape(channels, 7 * channels),
        biases[0][:, None],
        pool,
    )

    every_octant = share_octants(octants, group)
    parent = (first - 4) // 8

    def owner_of(block):
        below = starts[None, :] <= block[:, None]
        return (
            jnp.sum(below.astype(jnp.int32), axis=1) - 1,
            jnp.max(jnp.where(below, starts[None, :], 0), axis=1),
        )

    octant_ids = (parent - 2) * 8 + jnp.arange(64, dtype=jnp.int32)
    safe = jnp.clip(octant_ids, 0, total - 1)
    owner, start = owner_of(safe)
    octant_at = owner * slots + safe - start
    coarse_ids = parent - 1 + jnp.arange(6, dtype=jnp.int32)
    safe = jnp.clip(coarse_ids, 0, coarse_total - 1)
    owner, start = owner_of(safe * 8)
    cotangent_at = owner * coarse_slots + safe - (start + 7) // 8

    facts = jnp.stack(
        [
            chan,
            live,
            first - 4 - parent * 8,
            coarse_first - parent + 1,
            coarse_count,
            2 - parent,
            coarse_total - parent + 2,
        ]
    ).astype(jnp.int32)
    back_coarse = paired(full_coarse).transpose(2, 0, 1).reshape(channels, 7 * channels)
    back_fine = paired(full_fine).transpose(2, 0, 1).reshape(channels, 7 * channels)
    back_fine = lax.dynamic_slice_in_dim(back_fine, chan * group, group, 0)
    coarse_out, fine_grad, fine_wg, fine_bg, coarse_wg, coarse_bg = pl.pallas_call(
        backward_kernel,
        out_shape=(
            jax.ShapeDtypeStruct((coarse_slots, group, cells), BF16),
            jax.ShapeDtypeStruct((slots, group, cells), BF16),
            jax.ShapeDtypeStruct((7 * group, channels), F32),
            jax.ShapeDtypeStruct((group, channels), F32),
            jax.ShapeDtypeStruct((7 * group, channels), F32),
            jax.ShapeDtypeStruct((group, channels), F32),
        ),
        in_specs=[smem] * 4 + [vmem] * 10,
        out_specs=(vmem,) * 6,
        scratch_shapes=[
            pltpu.VMEM((7 * channels, cells), BF16),
            pltpu.VMEM((8, channels, cells), BF16),
            pltpu.VMEM((6, channels, cells), BF16),
            pltpu.VMEM((6, channels, cells), BF16),
            pltpu.VMEM((4, channels, cells), BF16),
            pltpu.VMEM((delta_rows + 1, channels, cells), BF16),
            pltpu.VMEM((group, cells), F32),
        ],
        compiler_params=pltpu.CompilerParams(vmem_limit_bytes=56 * 2**20),
    )(
        near_delta,
        facts,
        octant_at,
        cotangent_at,
        table,
        slope,
        every_octant,
        cotangents,
        full_coarse.transpose(1, 0, 2).reshape(channels, 7 * channels),
        biases[1][:, None],
        back_coarse,
        back_fine,
        place,
        spread,
    )
    partial = jnp.concatenate([fine_wg, fine_bg, coarse_wg, coarse_bg], axis=0)
    sums = sum_over_blocks(partial)
    half = 8 * group
    fine_norm = jnp.sqrt(total.astype(F32) * cells)
    coarse_norm = jnp.sqrt(coarse_total.astype(F32) * cells)
    fine_sums = sums[:half] / fine_norm
    coarse_sums = sums[half:] / coarse_norm

    def weight_part(part):
        return paired(part[: 7 * group].reshape(7, group, channels))

    return (
        coarse_out,
        fine_grad,
        weight_part(fine_sums),
        fine_sums[7 * group :, 0],
        weight_part(coarse_sums),
        coarse_sums[7 * group :, 0],
    )


def solution(mesh):
    placed = (
        P("blocks", "chan", None),
        P(),
        P(None, "chan", None),
        P("chan"),
        P(None, "chan", None),
        P("chan"),
        P("blocks", "chan", None),
    )
    return jax.shard_map(
        local,
        mesh=mesh,
        in_specs=placed,
        out_specs=(
            P("blocks", "chan", None),
            P("blocks", "chan", None),
            P(None, "chan", None),
            P("chan"),
            P(None, "chan", None),
            P("chan"),
        ),
        check_vma=False,
    )
```

```python
import jax
import jax.numpy as jnp
import numpy as np
from jax import lax
from jax.experimental import pallas as pl
from jax.experimental.pallas import tpu as pltpu
from jax.sharding import PartitionSpec as P

EDGE = 8
CELLS = EDGE**3
TAP_PAIRS = (0, 2, 1, 4, 3, 6, 5)
STRIDES = (1, 8, 64)
F32 = jnp.float32
BF16 = jnp.bfloat16


def octant_maps():
    z, y, x = np.meshgrid(*[np.arange(EDGE)] * 3, indexing="ij")
    spread = np.zeros((8, CELLS, CELLS), np.float32)
    pool = np.zeros((2, CELLS, 128), np.float32)
    place = np.zeros((2, 8, 128, CELLS), np.float32)
    fine = np.arange(CELLS)
    small = ((z // 2) * 16 + (y // 2) * 4 + x // 2).reshape(-1)
    for half in range(2):
        pool[half, fine, small + 64 * half] = 1.0
    for q in range(8):
        cz, cy, cx = z // 2 + 4 * (q // 4), y // 2 + 4 * (q // 2 % 2), x // 2 + 4 * (q % 2)
        coarse = (cz * 64 + cy * 8 + cx).reshape(-1)
        spread[q, coarse, fine] = 1.0
        for half in range(2):
            place[half, q, small + 64 * half, coarse] = 1.0
    return spread, pool, place


def paired(taps):
    return jnp.stack([taps[t] for t in TAP_PAIRS])


def sigmoid(v):
    return 1.0 / (1.0 + jnp.exp(-v))


def write_views(views, own, neighbours, width):
    lane = lax.broadcasted_iota(jnp.int32, own.shape, 1)
    views[0:width, :] = own
    wide = own.astype(F32)
    for axis in range(3):
        stride = STRIDES[axis]
        coord = lane // stride % EDGE
        for side in range(2):
            near, far = (0, EDGE - 1) if side == 0 else (EDGE - 1, 0)
            step = stride if side == 0 else CELLS - stride
            wrap = (CELLS - 7 * stride) if side == 0 else 7 * stride
            tap = 1 + 2 * axis + side
            other = neighbours[2 * axis + side]
            if other is None:
                out = jnp.where(coord == near, 0.0, pltpu.roll(wide, step, 1))
            else:
                mixed = jnp.where(coord == far, other.astype(F32), wide)
                out = pltpu.roll(mixed, step, 1)
                if step != wrap % CELLS:
                    out = jnp.where(coord == near, pltpu.roll(mixed, wrap, 1), out)
            views[tap * width : (tap + 1) * width, :] = out.astype(BF16)


def place_of(counts):
    me = lax.axis_index("blocks")

    def add(d, sums):
        held = counts[d]
        return sums[0] + jnp.where(d < me, held, 0), sums[1] + held

    first, total = lax.fori_loop(0, counts.shape[0], add, (jnp.int32(0), jnp.int32(0)))
    return first, counts[me], total


def owner_of(counts, block):
    def step(d, state):
        owner, start, here = state
        covers = here <= block
        return jnp.where(covers, d, owner), jnp.where(covers, here, start), here + counts[d]

    zero = jnp.int32(0)
    owner, start, _ = lax.fori_loop(0, counts.shape[0], step, (zero, zero, zero))
    return owner, start


def near_rows(block, total, row, absent):
    px, py = block % 2, block // 2 % 2
    tests = (
        (px == 1, -1), (px == 0, 1), (py == 1, -2), (py == 0, 2),
        (block >= 4, -4), (block + 4 < total, 4),
    )
    return [jnp.where(test, row(offset), absent) for test, offset in tests]


def forward_kernel(counts, table, weight, bias, pool, slope, octants, views):
    width = table.shape[1]
    first, live, total = place_of(counts)
    absent = table.shape[0] - 1
    slots = absent - 16

    def table_row(r):
        return jnp.where(r < 8 + live, r, jnp.minimum(r + slots - live, absent - 1))

    def row(j, carry):
        block = jnp.maximum(first - 4 + j, 0)
        near = near_rows(block, total, lambda offset: table_row(j + 4 + offset), absent)
        own = table[table_row(j + 4)]
        write_views(views, own, [table[r] for r in near], width)
        v = jnp.dot(weight[...], views[...], preferred_element_type=F32) + bias[...]
        s = sigmoid(v)
        slope[j] = s * (1.0 + v * (1.0 - s))

        @pl.when(jnp.logical_and(j >= 4, j < 20))
        def _():
            hidden = (v * s).astype(BF16)
            half = j % 2
            small = jnp.dot(hidden, pool[half], preferred_element_type=F32) * 0.125
            pair = (j - 4) // 2
            kept = jnp.where(half == 0, 0.0, octants[pair].astype(F32))
            octants[pair] = (kept + small).astype(BF16)

        return carry

    lax.fori_loop(0, slope.shape[0], row, 0)


def backward_kernel(
    counts, table, slope, octants, cotangent, forward_w, coarse_b, back_coarse_w, back_w,
    place, spread,
    coarse_out, fine_grad, fine_wg, fine_bg, coarse_wg, coarse_bg,
    views, coarse_in, coarse_act, coarse_delta, coarse_back, fine_delta, bias_sum,
):
    width = table.shape[1]
    slots, group = fine_grad.shape[0], fine_grad.shape[1]
    chan = lax.axis_index("chan")
    first, live, total = place_of(counts)
    parent = (first + 4) // 8 - 1
    parent0 = (first + 4) % 8
    coarse_first = (first + 7) // 8
    coarse_live = (first + live + 7) // 8 - coarse_first
    coarse_row = coarse_first - parent + 1
    coarse_begin, coarse_end = 2 - parent, total // 8 - parent + 2
    mine = pl.ds(pl.multiple_of(chan * group, group), group)

    def own_views():
        return jnp.concatenate(
            [views[pl.ds(pl.multiple_of(t * width + chan * group, group), group), :] for t in range(7)],
            axis=0,
        )

    def assemble(k, carry):
        cells = jnp.zeros((width, CELLS), F32)
        for q in range(8):
            block = jnp.clip((parent - 2 + k) * 8 + q, 0, total - 1)
            owner, start = owner_of(counts, block)
            slot = block - start
            both = jnp.concatenate(
                [octants[c, owner, slot // 2] for c in range(octants.shape[0])], axis=0
            )
            cells += jnp.dot(both, place[slot % 2, q], preferred_element_type=F32)
        inside = jnp.logical_and(k >= coarse_begin, k < coarse_end)
        coarse_in[k] = jnp.where(inside, cells, 0.0).astype(BF16)
        return carry

    lax.fori_loop(0, 8, assemble, 0)

    def coarse_forward(k, carry):
        write_views(
            views, coarse_in[k + 1], [None] * 4 + [coarse_in[k], coarse_in[k + 2]], width
        )
        v = jnp.dot(forward_w[...], views[...], preferred_element_type=F32) + coarse_b[...]
        s = sigmoid(v)
        coarse_act[k] = (v * s).astype(BF16)
        inside = jnp.logical_and(k + 1 >= coarse_begin, k + 1 < coarse_end)
        safe = jnp.clip(parent - 1 + k, 0, total // 8 - 1)
        owner, start = owner_of(counts, safe * 8)
        row = owner * coarse_out.shape[0] + safe - (start + 7) // 8
        delta = cotangent[row].astype(F32) * (s * (1.0 + v * (1.0 - s)))
        coarse_delta[k] = jnp.where(inside, delta, 0.0).astype(BF16)
        return carry

    lax.fori_loop(0, 6, coarse_forward, 0)
    for s in range(coarse_out.shape[0]):
        row = jnp.minimum(coarse_row + s, 5)
        kept = jnp.where(s < coarse_live, coarse_act[row, mine, :].astype(F32), 0.0)
        coarse_out[s] = kept.astype(BF16)

    coarse_wg[...] = jnp.zeros_like(coarse_wg)
    bias_sum[...] = jnp.zeros_like(bias_sum)

    def coarse_backward(k, carry):
        write_views(
            views,
            coarse_delta[k + 1],
            [None] * 4 + [coarse_delta[k], coarse_delta[k + 2]],
            width,
        )
        coarse_back[k] = jnp.dot(
            back_coarse_w[...], views[...], preferred_element_type=F32
        ).astype(BF16)
        row = k + 1

        @pl.when(jnp.logical_and(row >= coarse_row, row < coarse_row + coarse_live))
        def _():
            coarse_wg[...] += lax.dot_general(
                own_views(), coarse_in[k + 2], (((1,), (1,)), ((), ())), preferred_element_type=F32
            )
            bias_sum[...] += coarse_delta[row, mine, :].astype(F32)

        return carry

    lax.fori_loop(0, 4, coarse_backward, 0)
    coarse_bg[...] = jnp.broadcast_to(
        jnp.sum(bias_sum[...], axis=1, keepdims=True), coarse_bg.shape
    )

    def delta_row(j, carry):
        index = parent0 + j
        up = jnp.dot(coarse_back[index // 8], spread[index % 8], preferred_element_type=F32)
        fine_delta[j] = (up * 0.125 * slope[j]).astype(BF16)
        return carry

    lax.fori_loop(0, slope.shape[0], delta_row, 0)
    fine_delta[slope.shape[0]] = jnp.zeros((width, CELLS), BF16)
    fine_wg[...] = jnp.zeros_like(fine_wg)
    bias_sum[...] = jnp.zeros_like(bias_sum)

    def fine_row(r, carry):
        @pl.when(r < live)
        def _():
            near = near_rows(first + r, total, lambda offset: r + 4 + offset, slope.shape[0])
            write_views(views, fine_delta[r + 4], [fine_delta[n] for n in near], width)
            fine_grad[r] = jnp.dot(back_w[...], views[...], preferred_element_type=F32).astype(BF16)
            fine_wg[...] += lax.dot_general(
                own_views(), table[r + 8], (((1,), (1,)), ((), ())), preferred_element_type=F32
            )
            bias_sum[...] += fine_delta[r + 4, mine, :].astype(F32)

        @pl.when(r >= live)
        def _():
            fine_grad[r] = jnp.zeros((group, CELLS), BF16)

        return carry

    lax.fori_loop(0, fine_grad.shape[0], fine_row, 0)
    fine_bg[...] = jnp.broadcast_to(jnp.sum(bias_sum[...], axis=1, keepdims=True), fine_bg.shape)


def greet(axis):
    size, me = lax.axis_size(axis), lax.axis_index(axis)
    barrier = pltpu.get_barrier_semaphore()

    def one(d, carry):
        pl.semaphore_signal(
            barrier, inc=1, device_id={axis: (me + d) % size}, device_id_type=pl.DeviceIdType.MESH
        )
        return carry

    lax.fori_loop(1, size, one, 0)
    return size - 1


def push(src, dst, send_sem, recv_sem, axis, peer):
    return pltpu.make_async_remote_copy(
        src_ref=src,
        dst_ref=dst,
        send_sem=send_sem,
        recv_sem=recv_sem,
        device_id={axis: peer},
        device_id_type=pl.DeviceIdType.MESH,
    )


def exchange(axis, source, target, send_sem, recv_sem):
    size, me = lax.axis_size(axis), lax.axis_index(axis)

    def start(d, carry):
        peer = (me + d) % size
        push(source(peer), target(me, d), send_sem.at[d], recv_sem.at[d], axis, peer).start()
        return carry

    def finish(d, carry):
        peer = (me + d) % size
        giver = (me + size - d) % size
        push(source(peer), target(me, d), send_sem.at[d], recv_sem.at[d], axis, peer).wait_send()
        push(source(peer), target(giver, d), send_sem.at[d], recv_sem.at[d], axis, peer).wait_recv()
        return carry

    lax.fori_loop(1, size, start, 0)
    lax.fori_loop(1, size, finish, 0)


def chan_peers():
    me = lax.axis_index("chan")
    size = lax.axis_size("chan")
    far, near = (me + size // 2) % size, me + 1 - 2 * (me % 2)
    return me, far, near, (near + size // 2) % size


def greet_chan():
    _, far, near, _ = chan_peers()
    for peer in (far, near):
        pl.semaphore_signal(
            pltpu.get_barrier_semaphore(),
            inc=1,
            device_id={"chan": peer},
            device_id_type=pl.DeviceIdType.MESH,
        )
    return 2


def share_chan(parts, send_sem, recv_sem, base):
    me, far, near, near_far = chan_peers()

    def copy(n, k, held, peer):
        place = parts[n](held)
        at = base + 3 * n + k
        return push(place, place, send_sem.at[at], recv_sem.at[at], "chan", peer)

    def first():
        for n in range(len(parts)):
            copy(n, 0, me, far).start()
            copy(n, 1, me, near).start()

    def second():
        for n in range(len(parts)):
            copy(n, 0, far, far).wait_recv()
            copy(n, 2, far, near).start()
        return third

    def third():
        for n in range(len(parts)):
            copy(n, 1, near, near).wait_recv()
            copy(n, 2, near_far, near).wait_recv()
            copy(n, 0, me, far).wait_send()
            copy(n, 1, me, near).wait_send()
            copy(n, 2, far, near).wait_send()

    return first, second


def gather_kernel(
    tail, own, weight, bias, cotangent, table, weights, biases, cotangents,
    send_b, recv_b, send_c, recv_c,
):
    me, n = lax.axis_index("blocks"), lax.axis_size("blocks")
    chan = lax.axis_index("chan")
    slots, group, cells = own.shape
    after, before = (me + 1) % n, (me + n - 1) % n
    for peer in (after, before):
        pl.semaphore_signal(
            pltpu.get_barrier_semaphore(),
            inc=1,
            device_id={"blocks": peer},
            device_id_type=pl.DeviceIdType.MESH,
        )
    pl.semaphore_wait(pltpu.get_barrier_semaphore(), greet_chan() + 2)

    def lane(c):
        return pl.ds(pl.multiple_of(c * group, group), group)

    def rows(first, count):
        return lambda c: table.at[pl.ds(first, count), lane(c), :]

    lower, upper = rows(0, 8), rows(8 + slots, 8)
    down = push(own.at[pl.ds(0, 8)], upper(chan), send_b.at[0], recv_b.at[0], "blocks", before)
    up = push(tail, lower(chan), send_b.at[1], recv_b.at[1], "blocks", after)
    down.start()
    up.start()
    table[8 : 8 + slots, lane(chan), :] = own[...]
    weights[:, lane(chan), :] = weight[...]
    biases[chan] = bias[...]
    cotangents[:, lane(chan), :] = cotangent[...]
    table[16 + slots] = jnp.zeros(table.shape[1:], BF16)
    first, second = share_chan(
        [
            rows(8, slots),
            lambda c: weights.at[:, lane(c), :],
            lambda c: biases.at[c],
            lambda c: cotangents.at[:, lane(c), :],
        ],
        send_c, recv_c, 0,
    )
    halo_first, halo_second = share_chan([lower, upper], send_c, recv_c, 12)
    first()
    down.wait()
    up.wait()
    halo_first()
    third = second()
    halo_third = halo_second()
    third()
    halo_third()


def gather_start(tail, own, weight, bias, cotangent):
    width = lax.axis_size("chan")
    slots, group, cells = own.shape
    channels = group * width
    vmem = pl.BlockSpec(memory_space=pltpu.VMEM)
    return pl.pallas_call(
        gather_kernel,
        out_shape=(
            jax.ShapeDtypeStruct((slots + 17, channels, cells), BF16),
            jax.ShapeDtypeStruct((weight.shape[0], channels, channels), BF16),
            jax.ShapeDtypeStruct((width,) + bias.shape, F32),
            jax.ShapeDtypeStruct((cotangent.shape[0], channels, cells), BF16),
        ),
        in_specs=[vmem] * 5,
        out_specs=(vmem,) * 4,
        scratch_shapes=[
            pltpu.SemaphoreType.DMA((2,)),
            pltpu.SemaphoreType.DMA((2,)),
            pltpu.SemaphoreType.DMA((18,)),
            pltpu.SemaphoreType.DMA((18,)),
        ],
        compiler_params=pltpu.CompilerParams(
            collective_id=3, has_side_effects=True, vmem_limit_bytes=32 * 2**20
        ),
    )(tail, own, weight, bias, cotangent)


def octant_kernel(octants, out, send_b, recv_b, send_c, recv_c, own_sem):
    me, chan = lax.axis_index("blocks"), lax.axis_index("chan")
    group = out.shape[3]
    pl.semaphore_wait(pltpu.get_barrier_semaphore(), greet("blocks") + greet_chan())
    mine = octants.at[:, pl.ds(pl.multiple_of(chan * group, group), group), :]
    kept = pltpu.make_async_copy(mine, out.at[chan, me], own_sem)
    kept.start()
    exchange("blocks", lambda p: mine, lambda p, d: out.at[chan, p], send_b, recv_b)
    kept.wait()
    first, second = share_chan([lambda c: out.at[c]], send_c, recv_c, 0)
    first()
    second()()


def share_octants(octants, group):
    n, width = lax.axis_size("blocks"), lax.axis_size("chan")
    return pl.pallas_call(
        octant_kernel,
        out_shape=jax.ShapeDtypeStruct((width, n, octants.shape[0], group, 128), BF16),
        in_specs=[pl.BlockSpec(memory_space=pltpu.VMEM)],
        out_specs=pl.BlockSpec(memory_space=pltpu.VMEM),
        scratch_shapes=[
            pltpu.SemaphoreType.DMA((n,)),
            pltpu.SemaphoreType.DMA((n,)),
            pltpu.SemaphoreType.DMA((3,)),
            pltpu.SemaphoreType.DMA((3,)),
            pltpu.SemaphoreType.DMA,
        ],
        compiler_params=pltpu.CompilerParams(
            collective_id=1, has_side_effects=True, vmem_limit_bytes=32 * 2**20
        ),
    )(octants)


def sum_kernel(part, out, landed, send_a, recv_a, send_b, recv_b):
    me = lax.axis_index("blocks")
    size = part.shape[0]
    pl.semaphore_wait(pltpu.get_barrier_semaphore(), greet("blocks"))
    exchange("blocks", lambda p: part.at[p], lambda p, d: landed.at[d], send_a, recv_a)
    out[me] = lax.fori_loop(1, size, lambda d, total: total + landed[d], part[me])
    exchange("blocks", lambda p: out.at[me], lambda p, d: out.at[p], send_b, recv_b)


def sum_over_blocks(partial):
    n = lax.axis_size("blocks")
    rows, width = partial.shape
    shape = (n, rows // n, width)
    summed = pl.pallas_call(
        sum_kernel,
        out_shape=jax.ShapeDtypeStruct(shape, F32),
        in_specs=[pl.BlockSpec(memory_space=pltpu.VMEM)],
        out_specs=pl.BlockSpec(memory_space=pltpu.VMEM),
        scratch_shapes=[pltpu.VMEM(shape, F32)] + [pltpu.SemaphoreType.DMA((n,))] * 4,
        compiler_params=pltpu.CompilerParams(collective_id=2, has_side_effects=True),
    )(partial.reshape(shape))
    return summed.reshape(rows, width)


def local(
    fine_input, block_counts, fine_weight, fine_bias, coarse_weight, coarse_bias, coarse_cotangent
):
    slots, group, cells = fine_input.shape
    coarse_slots = coarse_cotangent.shape[0]
    channels = fine_weight.shape[2]
    device = lax.axis_index("blocks")
    chan = lax.axis_index("chan")
    live = block_counts[device]
    total = jnp.sum(block_counts)
    coarse_total = total // 8

    tail = lax.dynamic_slice_in_dim(fine_input, live - 8, 8, 0)
    table, weights, biases, cotangents = gather_start(
        tail,
        fine_input,
        jnp.concatenate([fine_weight, coarse_weight]),
        jnp.stack([fine_bias, coarse_bias]),
        coarse_cotangent,
    )
    biases = biases.transpose(1, 0, 2).reshape(2, channels)
    cotangents = lax.all_gather(cotangents, "blocks", axis=0, tiled=True)
    full_fine, full_coarse = weights[:7], weights[7:]

    spread, pool, place = (jnp.asarray(a, BF16) for a in octant_maps())
    delta_rows = slots + 8
    smem = pl.BlockSpec(memory_space=pltpu.SMEM)
    vmem = pl.BlockSpec(memory_space=pltpu.VMEM)
    slope, octants = pl.pallas_call(
        forward_kernel,
        out_shape=(
            jax.ShapeDtypeStruct((delta_rows, channels, cells), F32),
            jax.ShapeDtypeStruct((slots // 2, channels, 128), BF16),
        ),
        in_specs=[smem] + [vmem] * 4,
        out_specs=(vmem, vmem),
        scratch_shapes=[pltpu.VMEM((7 * channels, cells), BF16)],
        compiler_params=pltpu.CompilerParams(vmem_limit_bytes=40 * 2**20),
    )(
        block_counts,
        table,
        full_fine.transpose(1, 0, 2).reshape(channels, 7 * channels),
        biases[0][:, None],
        pool,
    )

    every_octant = share_octants(octants, group)
    back_coarse = paired(full_coarse).transpose(2, 0, 1).reshape(channels, 7 * channels)
    back_fine = paired(full_fine).transpose(2, 0, 1).reshape(channels, 7 * channels)
    back_fine = lax.dynamic_slice_in_dim(back_fine, chan * group, group, 0)
    coarse_out, fine_grad, fine_wg, fine_bg, coarse_wg, coarse_bg = pl.pallas_call(
        backward_kernel,
        out_shape=(
            jax.ShapeDtypeStruct((coarse_slots, group, cells), BF16),
            jax.ShapeDtypeStruct((slots, group, cells), BF16),
            jax.ShapeDtypeStruct((7 * group, channels), F32),
            jax.ShapeDtypeStruct((group, channels), F32),
            jax.ShapeDtypeStruct((7 * group, channels), F32),
            jax.ShapeDtypeStruct((group, channels), F32),
        ),
        in_specs=[smem] + [vmem] * 10,
        out_specs=(vmem,) * 6,
        scratch_shapes=[
            pltpu.VMEM((7 * channels, cells), BF16),
            pltpu.VMEM((8, channels, cells), BF16),
            pltpu.VMEM((6, channels, cells), BF16),
            pltpu.VMEM((6, channels, cells), BF16),
            pltpu.VMEM((4, channels, cells), BF16),
            pltpu.VMEM((delta_rows + 1, channels, cells), BF16),
            pltpu.VMEM((group, cells), F32),
        ],
        compiler_params=pltpu.CompilerParams(vmem_limit_bytes=56 * 2**20),
    )(
        block_counts,
        table,
        slope,
        every_octant,
        cotangents,
        full_coarse.transpose(1, 0, 2).reshape(channels, 7 * channels),
        biases[1][:, None],
        back_coarse,
        back_fine,
        place,
        spread,
    )
    partial = jnp.concatenate([fine_wg, fine_bg, coarse_wg, coarse_bg], axis=0)
    sums = sum_over_blocks(partial)
    half = 8 * group
    fine_norm = jnp.sqrt(total.astype(F32) * cells)
    coarse_norm = jnp.sqrt(coarse_total.astype(F32) * cells)
    fine_sums = sums[:half] / fine_norm
    coarse_sums = sums[half:] / coarse_norm

    def weight_part(part):
        return paired(part[: 7 * group].reshape(7, group, channels))

    return (
        coarse_out,
        fine_grad,
        weight_part(fine_sums),
        fine_sums[7 * group :, 0],
        weight_part(coarse_sums),
        coarse_sums[7 * group :, 0],
    )


def solution(mesh):
    placed = (
        P("blocks", "chan", None),
        P(),
        P(None, "chan", None),
        P("chan"),
        P(None, "chan", None),
        P("chan"),
        P("blocks", "chan", None),
    )
    return jax.shard_map(
        local,
        mesh=mesh,
        in_specs=placed,
        out_specs=(
            P("blocks", "chan", None),
            P("blocks", "chan", None),
            P(None, "chan", None),
            P("chan"),
            P(None, "chan", None),
            P("chan"),
        ),
        check_vma=False,
    )
```
